32 devices in a mesh: slab: 16 (over z, x, core), half: 2 (over y).
Axes of the slice: x: 2, y: 2, z: 4, core: 2. Of those that a mesh axis runs over, the one named last changes fastest.
Arguments:
- distributions: float32 [19, 32, 32, 256], P(None, 'slab', 'half'), may hold values from 0.02 to 0.1
- cell_states: float32 [2, 3, 169, 3072], P(None, None, None, ('slab', 'half')), may hold values from -6 to 6
- cell_counts: int32 [32], P(('slab', 'half')), may hold values from 16 to 96, as said below
- up_list: int32 [256], P(('slab', 'half')), may hold values from 0 to 96, as said below
- down_list: int32 [256], P(('slab', 'half')), may hold values from 0 to 96, as said below
- spread_sites: int32 [384, 3584], P(None, ('slab', 'half')), may hold values from 0 to 16383
- stiffness: float32 [169], replicated, may hold values from 0.1 to 2
- basis: float32 [169, 384], replicated, may hold values from -0.5 to 0.5
Outputs:
- new_distributions: float32 [19, 32, 32, 256], P(None, 'slab', 'half')
- moved_cells: float32 [2, 3, 169, 3584], P(None, None, None, ('slab', 'half'))
The draws below stay inside these ranges and needn't reach their ends.
Inputs may be any that keep to these rules, and one draw needn't show every extreme that they name: Each block keeps its cells in its first cell_counts slots. `up_list`: per block, the slots of cells crossing to slab s + 1 (wrapping); live entries come first, are distinct, lie below the block's count and differ from the block's down_list entries; the rest are 96. `down_list`: per block, the slots of cells crossing to slab s - 1 (wrapping); live entries come first, are distinct, lie below the block's count and differ from the block's up_list entries; the rest are 96.
All inputs are finite; a program needn't handle non-finite values.
Results may differ from the reference program's by a relative error of at most 0.0003.
Values sent between devices are 32-bit elements; how exact they have to be, the bound alone decides.
A program may use at most 64 MiB of HBM per device.

```python
import math
import jax
import jax.numpy as jnp
from jax import lax

SH = 169
Q = 384
CAP = 96
PX = 2
CY = 16
CZ = 256
MOVE = 8
SO = 112
SLABS = 16
HALVES = 2
GROUPS = 32
NX = 32
NY = 32
NZ = 256
CELLS = 3072
SLOTS = 3584


def shared_counts(key):
    key = jax.random.fold_in(key, 101)
    pick_key, level_key = jax.random.split(key)
    group_ids = jnp.arange(GROUPS, dtype=jnp.int32)
    level = jax.random.randint(level_key, (GROUPS,), 0, 17)
    lowest = 2 * MOVE
    counts = lowest + (CAP - lowest) * level * level // 256
    picked = jax.random.randint(pick_key, (), 0, GROUPS)
    counts = jnp.where(group_ids == picked, CAP, counts)
    counts = jnp.where(group_ids == (picked + 1) % GROUPS, lowest, counts)
    return counts.astype(jnp.int32)


def shared_lists(key):
    counts = shared_counts(key)
    key = jax.random.fold_in(key, 202)
    score_key, up_key, down_key, pick_key = jax.random.split(key, 4)
    slot_ids = jnp.arange(CAP, dtype=jnp.int32)
    group_ids = jnp.arange(GROUPS, dtype=jnp.int32)
    picked = jax.random.randint(pick_key, (), 0, GROUPS)
    second = (picked + 1) % GROUPS
    special = ((group_ids == picked) | (group_ids == second))[:, None] & (slot_ids[None, :] == 0)
    noise = jax.random.randint(score_key, (GROUPS, CAP), 0, 2 ** 19)
    score = noise * CAP + slot_ids[None, :] + jnp.where(slot_ids[None, :] >= counts[:, None], 2 ** 30, 0)
    score = jnp.where(special, -1, score)
    ordered = jnp.argsort(score, axis=1)[:, :2 * MOVE].astype(jnp.int32)
    swap_rows = (group_ids == second)[:, None]
    first_part = jnp.where(swap_rows, ordered[:, MOVE:], ordered[:, :MOVE])
    other_part = jnp.where(swap_rows, ordered[:, :MOVE], ordered[:, MOVE:])
    up_length = jax.random.randint(up_key, (GROUPS,), 1, MOVE + 1)
    down_length = jax.random.randint(down_key, (GROUPS,), 1, MOVE + 1)
    up_length = jnp.where(group_ids == picked, MOVE, jnp.where(group_ids == second, 1, up_length))
    down_length = jnp.where(group_ids == second, MOVE, jnp.where(group_ids == picked, 1, down_length))
    lane_ids = jnp.arange(MOVE, dtype=jnp.int32)
    upward = jnp.where(lane_ids[None, :] < up_length[:, None], first_part, CAP)
    downward_source = jnp.where(swap_rows, ordered[:, :MOVE], other_part)
    downward = jnp.where(lane_ids[None, :] < down_length[:, None], downward_source, CAP)
    upward = jnp.where(swap_rows, jnp.where(lane_ids[None, :] < up_length[:, None], ordered[:, MOVE:], CAP), upward)
    return (upward.reshape(-1).astype(jnp.int32), downward.reshape(-1).astype(jnp.int32))


def draw_cell_counts(key, part):
    return shared_counts(key)


def draw_up_list(key, part):
    return shared_lists(key)[0]


def draw_down_list(key, part):
    return shared_lists(key)[1]


def touch_ends(values, own_key, smallest, largest):
    place = [jax.random.randint(jax.random.fold_in(own_key, axis), (), 0, length) for axis, length in enumerate(values.shape)]
    longest = values.shape.index(max(values.shape))
    next_to = place[:longest] + [(place[longest] + 1) % values.shape[longest]] + place[longest + 1:]
    return values.at[tuple(place)].set(smallest).at[tuple(next_to)].set(largest)


def steps_of(own_key, dims, cuts, least, largest):
    def one(axis_at, shards_of):
        draws = jax.random.uniform(jax.random.fold_in(jax.random.fold_in(own_key, 6), axis_at), (shards_of,), jnp.float32, least / len(cuts), largest / len(cuts))
        return jnp.repeat(jnp.exp(draws), dims[axis_at] // shards_of).reshape((-1,) + (1,) * (len(dims) - axis_at - 1))

    factor_of = one(*cuts[0])
    for cut in cuts[1:]:
        factor_of = factor_of * one(*cut)
    return factor_of


def centred(own_key, shape, scale, bound, cuts=(), held_as=jnp.bfloat16):
    values = scale * jax.random.normal(own_key, shape, jnp.float32)
    if cuts:
        values = values * steps_of(own_key, shape, cuts, -0.22, 0.18)
    return jnp.clip(values, -bound, bound).astype(held_as)


def setup_inputs(seed: int = 0) -> dict:
    seeds = jax.random.split(jax.random.key(seed), 9)
    return {
        "distributions": jnp.clip(jnp.exp(math.log(0.1) - 1.609438 * jax.random.uniform(seeds[0], (19, NX, NY, NZ), jnp.float32) ** steps_of(seeds[0], (19, NX, NY, NZ), ((1, 16), (2, 2)), -0.2, 0.2)), 0.02, 0.1),
        "cell_states": centred(seeds[1], (2, 3, SH, CELLS), 1.0, 6.0, ((3, 32),), jnp.float32),
        "cell_counts": draw_cell_counts(jax.random.fold_in(seeds[8], 71), 0),
        "up_list": draw_up_list(jax.random.fold_in(seeds[8], 71), 0),
        "down_list": draw_down_list(jax.random.fold_in(seeds[8], 71), 0),
        "spread_sites": touch_ends(jax.random.randint(seeds[5], (Q, SLOTS), 0, (PX + 2) * CY * CZ), jax.random.fold_in(seeds[5], 1), 0, ((PX + 2) * CY * CZ) - 1).astype(jnp.int32),
        "stiffness": jnp.clip(jnp.exp(jax.random.uniform(seeds[6], (SH,), jnp.float32, math.log(0.1), math.log(2.0))), 0.1, 2.0),
        "basis": centred(seeds[7], (SH, Q), SH ** -0.5, 0.5, (), jnp.float32),
    }


full_precision = lax.Precision.HIGHEST
relaxation_time = 0.8
membrane_tension = 0.5
spread_weight = 0.05
lattice_velocities = ((0, 0, 0), (1, 0, 0), (-1, 0, 0), (0, 1, 0), (0, -1, 0), (0, 0, 1), (0, 0, -1),
                      (1, 1, 0), (-1, -1, 0), (1, -1, 0), (-1, 1, 0), (1, 0, 1), (-1, 0, -1),
                      (1, 0, -1), (-1, 0, 1), (0, 1, 1), (0, -1, -1), (0, 1, -1), (0, -1, 1))
lattice_weights = (1.0 / 3.0,) + (1.0 / 18.0,) * 6 + (1.0 / 36.0,) * 12
opposite_of = (0, 2, 1, 4, 3, 6, 5, 8, 7, 10, 9, 12, 11, 14, 13, 16, 15, 18, 17)


def point_forces(cells, stiffness, basis):
    current = cells[0]
    rest_shape = cells[1]
    positions = jnp.einsum('kq,ckb->cqb', basis, current, precision=full_precision)
    elastic = jnp.einsum('kq,ckb->cqb', basis, stiffness[None, :, None] * (rest_shape - current), precision=full_precision)
    radial = positions - jnp.mean(positions, axis=1, keepdims=True)
    squared = jnp.sum(radial * radial, axis=0)
    mean_square = jnp.mean(squared, axis=0) + 1e-5
    stretch = squared / mean_square - 1.0
    return elastic - membrane_tension * stretch[None] * radial


def collide(populations, force):
    velocity_table = jnp.array(lattice_velocities, jnp.float32)
    weight_table = jnp.array(lattice_weights, jnp.float32)[:, None, None, None]
    density = jnp.sum(populations, axis=0)
    momentum = jnp.einsum('ic,ixyz->cxyz', velocity_table, populations, precision=full_precision)
    flow_speed = (momentum + 0.5 * force) / density
    projected = jnp.einsum('ic,cxyz->ixyz', velocity_table, flow_speed, precision=full_precision)
    force_along = jnp.einsum('ic,cxyz->ixyz', velocity_table, force, precision=full_precision)
    speed_square = jnp.sum(flow_speed * flow_speed, axis=0)
    power_term = jnp.sum(flow_speed * force, axis=0)
    balance = weight_table * density * (1.0 + 3.0 * projected + 4.5 * projected * projected - 1.5 * speed_square)
    source = weight_table * (3.0 * (force_along - power_term) + 9.0 * projected * force_along)
    return populations - (populations - balance) / relaxation_time + (1.0 - 0.5 / relaxation_time) * source


def stream(relaxed):
    rows_total = relaxed.shape[2]
    row_ids = jnp.arange(rows_total)
    result = []
    for velocity_id, (step_x, step_y, step_z) in enumerate(lattice_velocities):
        shifted = jnp.roll(relaxed[velocity_id], (step_x, step_y, step_z), axis=(0, 1, 2))
        inside = ((row_ids - step_y >= 0) & (row_ids - step_y < rows_total))[None, :, None]
        result.append(jnp.where(inside, shifted, relaxed[opposite_of[velocity_id]]))
    return jnp.stack(result)


def reference(distributions, cell_states, cell_counts, up_list, down_list, spread_sites, stiffness, basis):
    slot_ids = jnp.arange(CAP, dtype=jnp.int32)

    def cells_of(group_id):
        return lax.dynamic_slice_in_dim(cell_states, group_id * CAP, CAP, 3)

    def list_of(table, group_id):
        return lax.dynamic_slice_in_dim(table, group_id * MOVE, MOVE, 0)

    def chosen(cell_block, entries):
        picked = jnp.take(cell_block, jnp.minimum(entries, CAP - 1), axis=3)
        return picked * (entries < CAP).astype(cell_block.dtype)

    def visit_group(force_field, group_id):
        slab_id = group_id // HALVES
        half_id = group_id % HALVES
        lower_group = ((slab_id - 1) % SLABS) * HALVES + half_id
        upper_group = ((slab_id + 1) % SLABS) * HALVES + half_id
        own_cells = cells_of(group_id)
        leaving = jnp.concatenate([list_of(up_list, group_id), list_of(down_list, group_id)])
        keep_mask = (slot_ids < cell_counts[group_id]) & ~jnp.any(slot_ids[:, None] == leaving[None, :], axis=1)
        kept_cells = own_cells * keep_mask.astype(own_cells.dtype)
        moved_block = jnp.concatenate([kept_cells,
                                       chosen(cells_of(lower_group), list_of(up_list, lower_group)),
                                       chosen(cells_of(upper_group), list_of(down_list, upper_group))], axis=3)
        pushes = point_forces(moved_block, stiffness, basis)
        site_block = lax.dynamic_slice_in_dim(spread_sites, group_id * SO, SO, 1)
        plane_index = site_block // (CY * CZ)
        row_index = (site_block // CZ) % CY
        column = site_block % CZ
        global_plane = (slab_id * PX + plane_index - 1) % NX
        target = (global_plane * NY + half_id * CY + row_index) * NZ + column
        force_field = force_field.at[:, target.reshape(-1)].add(pushes.reshape(3, -1))
        return force_field, moved_block

    empty_field = jnp.zeros((3, NX * NY * NZ), jnp.float32)
    force_field, moved_all = lax.scan(visit_group, empty_field, jnp.arange(GROUPS, dtype=jnp.int32))
    force_density = (spread_weight * force_field).reshape(3, NX, NY, NZ)
    new_distributions = stream(collide(distributions, force_density))
    moved_cells = jnp.moveaxis(moved_all, 0, 3).reshape(2, 3, SH, GROUPS * SO)
    return new_distributions, moved_cells
```

```python
import math

import jax
import jax.numpy as jnp
from jax import lax
from jax.sharding import PartitionSpec as P

full_precision = lax.Precision.HIGHEST
relaxation_time = 0.8
membrane_tension = 0.5
spread_weight = 0.05
lattice_velocities = (
    (0, 0, 0),
    (1, 0, 0),
    (-1, 0, 0),
    (0, 1, 0),
    (0, -1, 0),
    (0, 0, 1),
    (0, 0, -1),
    (1, 1, 0),
    (-1, -1, 0),
    (1, -1, 0),
    (-1, 1, 0),
    (1, 0, 1),
    (-1, 0, -1),
    (1, 0, -1),
    (-1, 0, 1),
    (0, 1, 1),
    (0, -1, -1),
    (0, 1, -1),
    (0, -1, 1),
)
lattice_weights = (1.0 / 3.0,) + (1.0 / 18.0,) * 6 + (1.0 / 36.0,) * 12
opposite_of = (0, 2, 1, 4, 3, 6, 5, 8, 7, 10, 9, 12, 11, 14, 13, 16, 15, 18, 17)


def padded_2(cells, sides, width):
    for axis, dim in sides:
        count = lax.axis_size(axis)
        head = lax.slice_in_dim(cells, 0, width, axis=dim)
        tail = lax.slice_in_dim(cells, cells.shape[dim] - width, cells.shape[dim], axis=dim)
        cells = jnp.concatenate(
            [
                lax.ppermute(tail, axis, [(i, (i + 1) % count) for i in range(count)]),
                cells,
                lax.ppermute(head, axis, [((i + 1) % count, i) for i in range(count)]),
            ],
            axis=dim,
        )
    return cells


def from_behind(array, axis, by):
    devices = lax.axis_size(axis)
    return lax.ppermute(array, axis, [(i, (i + by) % devices) for i in range(devices)])


def point_forces(cells, stiffness, basis):
    current = cells[0]
    rest_shape = cells[1]
    positions = jnp.einsum("kq,ckb->cqb", basis, current, precision=full_precision)
    elastic = jnp.einsum(
        "kq,ckb->cqb",
        basis,
        stiffness[None, :, None] * (rest_shape - current),
        precision=full_precision,
    )
    radial = positions - jnp.mean(positions, axis=1, keepdims=True)
    squared = jnp.sum(radial * radial, axis=0)
    mean_square = jnp.mean(squared, axis=0) + 1e-05
    stretch = squared / mean_square - 1.0
    return elastic - membrane_tension * stretch[None] * radial


def forces_of(cells, stiffness, basis):
    result = point_forces(cells, stiffness, basis)
    return result


def chosen(values, entries, capacity):
    selector = (jnp.arange(capacity, dtype=jnp.int32)[:, None] == entries[None, :]).astype(
        jnp.float32
    )
    return jnp.einsum("...s,sm->...m", values, selector, precision=full_precision)


def spread_points(pushes, spread_sites, site_rows, columns):
    point_rows = pushes.shape[1]
    slot_total = pushes.shape[2]
    group_rows = math.gcd(point_rows, 32)
    row_table = jnp.arange(site_rows, dtype=jnp.int32)
    column_table = jnp.arange(columns, dtype=jnp.int32)
    coarse = lax.reduce_precision(pushes, 8, 7)
    parts = jnp.concatenate([coarse, pushes - coarse], axis=0).astype(jnp.bfloat16)
    pieces = parts.shape[0]

    def visit_rows(turn, total):
        site_piece = lax.dynamic_slice_in_dim(
            spread_sites, turn * group_rows, group_rows, 0
        ).reshape(-1)
        force_piece = lax.dynamic_slice_in_dim(parts, turn * group_rows, group_rows, 1).reshape(
            pieces, group_rows * slot_total
        )
        row_hot = row_table[:, None] == (site_piece // columns)[None, :]
        column_hot = ((site_piece % columns)[:, None] == column_table[None, :]).astype(jnp.bfloat16)
        weighted = jnp.where(row_hot[None], force_piece[:, None, :], jnp.bfloat16(0))
        return total + jnp.einsum(
            "crn,nz->crz", weighted, column_hot, preferred_element_type=jnp.float32
        )

    empty_total = jnp.zeros((pieces, site_rows, columns), jnp.float32)
    total = lax.fori_loop(0, point_rows // group_rows, visit_rows, empty_total)
    return total[: pieces // 2] + total[pieces // 2 :]


def collide(populations, force):
    velocity_table = jnp.array(lattice_velocities, jnp.float32)
    weight_table = jnp.array(lattice_weights, jnp.float32)[:, None, None, None]
    density = jnp.sum(populations, axis=0)
    momentum = jnp.einsum("ic,ixyz->cxyz", velocity_table, populations, precision=full_precision)
    flow_speed = (momentum + 0.5 * force) / density
    projected = jnp.einsum("ic,cxyz->ixyz", velocity_table, flow_speed, precision=full_precision)
    force_along = jnp.einsum("ic,cxyz->ixyz", velocity_table, force, precision=full_precision)
    speed_square = jnp.sum(flow_speed * flow_speed, axis=0)
    power_term = jnp.sum(flow_speed * force, axis=0)
    balance = (
        weight_table
        * density
        * (1.0 + 3.0 * projected + 4.5 * projected * projected - 1.5 * speed_square)
    )
    source = weight_table * (3.0 * (force_along - power_term) + 9.0 * projected * force_along)
    return (
        populations
        - (populations - balance) / relaxation_time
        + (1.0 - 0.5 / relaxation_time) * source
    )


def stream_local(relaxed):
    planes = relaxed.shape[1]
    rows_here = relaxed.shape[2]
    row_ids = lax.axis_index("half") * rows_here + jnp.arange(rows_here, dtype=jnp.int32)
    rows_total = rows_here * lax.axis_size("half")
    padded = padded_2(relaxed, (("slab", 1), ("half", 2)), 1)
    shifted = [
        jnp.roll(
            padded[vid, 1 - vel[0] : 1 - vel[0] + planes, 1 - vel[1] : 1 - vel[1] + rows_here],
            vel[2],
            axis=2,
        )
        for vid, vel in enumerate(lattice_velocities)
    ]
    result = []
    for velocity_id, vel in enumerate(lattice_velocities):
        inside = ((row_ids - vel[1] >= 0) & (row_ids - vel[1] < rows_total))[None, :, None]
        result.append(jnp.where(inside, shifted[velocity_id], relaxed[opposite_of[velocity_id]]))
    return jnp.stack(result)


def shards(
    distributions, cell_states, cell_counts, up_list, down_list, spread_sites, stiffness, basis
):
    capacity = cell_states.shape[3]
    planes = distributions.shape[1]
    rows_here = distributions.shape[2]
    columns = distributions.shape[3]
    held_count = cell_counts[0]
    slot_ids = jnp.arange(capacity, dtype=jnp.int32)
    leaving = jnp.concatenate([up_list, down_list])
    keep_mask = (slot_ids < held_count) & ~jnp.any(slot_ids[:, None] == leaving[None, :], axis=1)
    kept_cells = cell_states * keep_mask.astype(jnp.float32)
    from_lower = from_behind(chosen(cell_states, up_list, capacity), "slab", 1)
    from_upper = from_behind(chosen(cell_states, down_list, capacity), "slab", -1)
    moved_cells = jnp.concatenate([kept_cells, from_lower, from_upper], axis=3)
    arriving = point_forces(jnp.concatenate([from_lower, from_upper], axis=3), stiffness, basis)
    pushes = jnp.concatenate([forces_of(kept_cells, stiffness, basis), arriving], axis=2)
    extended = spread_points(pushes, spread_sites, (planes + 2) * rows_here, columns)
    extended = extended.reshape(3, planes + 2, rows_here, columns)
    from_below = from_behind(extended[:, planes + 1], "slab", 1)
    from_above = from_behind(extended[:, 0], "slab", -1)
    summed_force = (
        extended[:, 1 : planes + 1].at[:, 0].add(from_below).at[:, planes - 1].add(from_above)
    )
    force_density = spread_weight * summed_force
    relaxed = collide(distributions, force_density)
    new_distributions = stream_local(relaxed)
    return (new_distributions, moved_cells)


def solution(mesh):
    placed = (
        P(None, "slab", "half", None),
        P(None, None, None, ("slab", "half")),
        P(("slab", "half")),
        P(("slab", "half")),
        P(("slab", "half")),
        P(None, ("slab", "half")),
        P(),
        P(),
    )
    return jax.shard_map(
        shards,
        mesh=mesh,
        in_specs=placed,
        out_specs=(P(None, "slab", "half", None), P(None, None, None, ("slab", "half"))),
        check_vma=False,
    )
```

```python
import jax
import jax.numpy as jnp
from jax import lax
from jax.experimental import pallas as pl
from jax.experimental.pallas import tpu as pltpu
from jax.sharding import PartitionSpec as P

full_precision = lax.Precision.HIGHEST
relaxation_time = 0.8
membrane_tension = 0.5
spread_weight = 0.05
lattice_velocities = (
    (0, 0, 0),
    (1, 0, 0),
    (-1, 0, 0),
    (0, 1, 0),
    (0, -1, 0),
    (0, 0, 1),
    (0, 0, -1),
    (1, 1, 0),
    (-1, -1, 0),
    (1, -1, 0),
    (-1, 1, 0),
    (1, 0, 1),
    (-1, 0, -1),
    (1, 0, -1),
    (-1, 0, 1),
    (0, 1, 1),
    (0, -1, -1),
    (0, 1, -1),
    (0, -1, 1),
)
lattice_weights = (1.0 / 3.0,) + (1.0 / 18.0,) * 6 + (1.0 / 36.0,) * 12
opposite_of = (0, 2, 1, 4, 3, 6, 5, 8, 7, 10, 9, 12, 11, 14, 13, 16, 15, 18, 17)
all_ids = tuple(range(19))
ahead_ids = tuple(i for i in all_ids if lattice_velocities[i][0] == 1)
behind_ids = tuple(i for i in all_ids if lattice_velocities[i][0] == -1)
rising_ids = tuple(i for i in all_ids if lattice_velocities[i][1] == 1)
falling_ids = tuple(opposite_of[i] for i in rising_ids)
level_ids = tuple(i for i in all_ids if lattice_velocities[i][1] == 0)


def total_of(terms):
    result = None
    for sign, value in terms:
        if sign == 0:
            continue
        if result is None:
            result = value if sign > 0 else -value
        else:
            result = result + value if sign > 0 else result - value
    return result


def moments_of(populations):
    density = total_of([(1, f) for f in populations])
    momentum = [
        total_of([(lattice_velocities[i][axis], populations[i]) for i in all_ids])
        for axis in range(3)
    ]
    return [density] + momentum


def collide(ids, population_of, moments, force):
    density = moments[0]
    inverse = 1.0 / density
    speed = [(moments[1 + a] + 0.5 * force[a]) * inverse for a in range(3)]
    speed_square = speed[0] * speed[0] + speed[1] * speed[1] + speed[2] * speed[2]
    power = speed[0] * force[0] + speed[1] * force[1] + speed[2] * force[2]
    base = 1.0 - 1.5 * speed_square
    result = {}
    for i in ids:
        vel = lattice_velocities[i]
        weight = lattice_weights[i]
        f = population_of(i)
        if i == 0:
            balance = (weight * density) * base
            source = (-3.0 * weight) * power
        else:
            projected = total_of(list(zip(vel, speed)))
            along = total_of(list(zip(vel, force)))
            balance = (weight * density) * (base + projected * (3.0 + 4.5 * projected))
            source = weight * (3.0 * (along - power) + 9.0 * projected * along)
        result[i] = (
            f - (f - balance) / relaxation_time + (1.0 - 0.5 / relaxation_time) * source
        )
    return result


def step_kernel(
    count_ref,
    up_ref,
    down_ref,
    dist_ref,
    cells_ref,
    sites_ref,
    stiff_ref,
    basis_ref,
    out_ref,
    moved_ref,
    basis_pad,
    stiff_pad,
    pushes,
    spread_acc,
    cell_send,
    cell_recv,
    halo_send,
    halo_recv,
    force_own,
    force_recv,
    row_send,
    row_recv,
    own_moments,
    relaxed,
    send_sems,
    recv_sems,
):
    slab = lax.axis_index("slab")
    half = lax.axis_index("half")
    slabs = lax.axis_size("slab")
    above = {"slab": lax.rem(slab + 1, slabs), "half": half}
    below = {"slab": lax.rem(slab + slabs - 1, slabs), "half": half}
    across = {"slab": slab, "half": 1 - half}
    mesh_ids = pl.DeviceIdType.MESH

    planes, rows, columns = dist_ref.shape[1:]
    coefficients, points = basis_ref.shape
    capacity, width = cells_ref.shape[2:]
    move = up_ref.shape[0]
    slots = sites_ref.shape[0]

    barrier = pltpu.get_barrier_semaphore()
    for device in (above, below, across):
        pl.semaphore_signal(barrier, inc=1, device_id=device, device_id_type=mesh_ids)

    def remote(at, source, target, device):
        return pltpu.make_async_remote_copy(
            src_ref=source,
            dst_ref=target,
            send_sem=send_sems.at[at],
            recv_sem=recv_sems.at[at],
            device_id=device,
            device_id_type=mesh_ids,
        )

    entry_ids = lax.broadcasted_iota(jnp.int32, (2 * move, capacity), 0)
    slot_ids = lax.broadcasted_iota(jnp.int32, (2 * move, capacity), 1)
    entries = jnp.zeros((2 * move, capacity), jnp.int32)
    for k in range(move):
        entries = jnp.where(entry_ids == k, up_ref[k], entries)
        entries = jnp.where(entry_ids == move + k, down_ref[k], entries)
    selector = (entries == slot_ids).astype(jnp.float32)
    for w in range(2):
        for c in range(3):
            picked = jnp.dot(
                selector,
                cells_ref[w, c],
                precision=full_precision,
                preferred_element_type=jnp.float32,
            )
            cell_send[0, w, c] = picked[:move]
            cell_send[1, w, c] = picked[move:]

    pl.semaphore_wait(barrier, 3)
    cells_up = remote(0, cell_send.at[0], cell_recv.at[0], above)
    cells_down = remote(1, cell_send.at[1], cell_recv.at[1], below)
    cells_up.start()
    cells_down.start()

    for p in range(planes):
        moments = moments_of([dist_ref[i, p] for i in all_ids])
        for k in range(4):
            own_moments[k, p] = moments[k]
    for side, (p, ids) in enumerate(((planes - 1, ahead_ids), (0, behind_ids))):
        for k in range(4):
            halo_send[side, k] = own_moments[k, p]
        for k, i in enumerate(ids):
            halo_send[side, 4 + k] = dist_ref[i, p]
    halo_up = remote(2, halo_send.at[0], halo_recv.at[0], above)
    halo_down = remote(3, halo_send.at[1], halo_recv.at[1], below)
    halo_up.start()
    halo_down.start()

    basis_pad[...] = jnp.zeros_like(basis_pad)
    basis_pad[:coefficients, :] = basis_ref[...]
    stiff_pad[...] = jnp.zeros_like(stiff_pad)
    stiff_pad[:, :coefficients] = stiff_ref[...]

    held = lax.broadcasted_iota(jnp.int32, (capacity, width), 0)
    gone = held >= count_ref[0]
    for k in range(move):
        gone = gone | (held == up_ref[k]) | (held == down_ref[k])
    for w in range(2):
        for c in range(3):
            moved_ref[w, c, :capacity, :] = jnp.where(gone, 0.0, cells_ref[w, c])

    def point_forces(first, count):
        current = [moved_ref[0, c, first : first + count, :] for c in range(3)]
        rest = [moved_ref[1, c, first : first + count, :] for c in range(3)]
        stiffness = stiff_pad[...]
        strain = [stiffness * (r - x) for r, x in zip(rest, current)]
        product = jnp.dot(
            jnp.concatenate(current + strain, axis=0),
            basis_pad[...],
            precision=full_precision,
            preferred_element_type=jnp.float32,
        )
        parts = [product[k * count : (k + 1) * count] for k in range(6)]
        radial = [x - jnp.sum(x, axis=1, keepdims=True) / points for x in parts[:3]]
        squared = radial[0] * radial[0] + radial[1] * radial[1] + radial[2] * radial[2]
        mean_square = jnp.sum(squared, axis=1, keepdims=True) / points + 1e-05
        factor = membrane_tension * (squared / mean_square - 1.0)
        for c in range(3):
            pushes[c, first : first + count, :] = parts[3 + c] - factor * radial[c]

    group = 8
    site_rows = spread_acc.shape[0] // 6
    shift = columns.bit_length() - 1
    zero = jnp.zeros((), jnp.bfloat16)

    def spread(turn, carry):
        start = pl.multiple_of(turn * group, group)
        sites = sites_ref[pl.ds(start, group), :]
        row_of = (sites >> shift).astype(jnp.float32)
        column_of = (sites & (columns - 1)).astype(jnp.float32)
        values = []
        for c in range(3):
            push = pushes[c, pl.ds(start, group), :]
            coarse = push.astype(jnp.bfloat16).astype(jnp.float32)
            values += [coarse, push - coarse]
        row_ids = lax.broadcasted_iota(jnp.int32, (site_rows, points), 0)
        row_ids = row_ids.astype(jnp.float32).astype(jnp.bfloat16)
        column_ids = lax.broadcasted_iota(jnp.int32, (columns, points), 0)
        column_ids = column_ids.astype(jnp.float32).astype(jnp.bfloat16)

        def tall(array, k, height):
            tile = jnp.broadcast_to(array[k : k + 1], (16, points)).astype(jnp.bfloat16)
            return jnp.concatenate([tile] * (height // 16), axis=0)

        weighted = []
        hot = []
        for k in range(group):
            mask = row_ids == tall(row_of, k, site_rows)
            weighted.append(
                jnp.concatenate(
                    [jnp.where(mask, tall(v, k, site_rows), zero) for v in values], axis=0
                )
            )
            hot.append(
                jnp.where(
                    column_ids == tall(column_of, k, columns), jnp.ones((), jnp.bfloat16), zero
                )
            )
        spread_acc[...] += lax.dot_general(
            jnp.concatenate(weighted, axis=1),
            jnp.concatenate(hot, axis=1),
            (((1,), (1,)), ((), ())),
            preferred_element_type=jnp.float32,
        )
        return carry

    spread_acc[...] = jnp.zeros_like(spread_acc)
    point_forces(0, capacity)
    lax.fori_loop(0, capacity // group, spread, 0)

    cells_up.wait()
    cells_down.wait()
    for w in range(2):
        for c in range(3):
            moved_ref[w, c, capacity : capacity + move, :] = cell_recv[0, w, c]
            moved_ref[w, c, capacity + move :, :] = cell_recv[1, w, c]
    point_forces(capacity, 2 * move)
    lax.fori_loop(capacity // group, slots // group, spread, 0)

    for c in range(3):
        first = 2 * c * site_rows
        whole = spread_acc[first : first + site_rows, :] + (
            spread_acc[first + site_rows : first + 2 * site_rows, :]
        )
        whole = (spread_weight * whole).reshape(2, 2, rows, columns)
        force_own[0, c] = whole[0]
        force_own[1, c] = whole[1]
    force_down = remote(4, force_own.at[0], force_recv.at[1], below)
    force_up = remote(5, force_own.at[1], force_recv.at[0], above)
    force_down.start()
    force_up.start()
    halo_up.wait()
    halo_down.wait()
    force_down.wait()
    force_up.wait()

    for plane in range(planes + 2):
        side, at = divmod(plane, 2)
        force = [force_own[side, c, at] + force_recv[side, c, at] for c in range(3)]
        if plane == 0 or plane == planes + 1:
            which = 0 if plane == 0 else 1
            ids = ahead_ids if plane == 0 else behind_ids
            moments = [halo_recv[which, k] for k in range(4)]
            found = collide(
                ids, lambda i: halo_recv[which, 4 + ids.index(i)], moments, force
            )
        else:
            moments = [own_moments[k, plane - 1] for k in range(4)]
            found = collide(all_ids, lambda i: dist_ref[i, plane - 1], moments, force)
        for i, value in found.items():
            relaxed[i, plane] = value

    def carried(i, p):
        vel = lattice_velocities[i]
        value = relaxed[i, p + 1 - vel[0]]
        if vel[2]:
            value = pltpu.roll(value, vel[2] % columns, 1)
        return value

    row_ids = lax.broadcasted_iota(jnp.int32, (rows, columns), 0)
    lower_half = jnp.full((1, columns), half, jnp.int32) == 0
    for j, (i, o) in enumerate(zip(rising_ids, falling_ids)):
        for p in range(planes):
            rising = carried(i, p)
            falling = carried(o, p)
            at = j * planes + p
            row_send[at : at + 1, :] = jnp.where(lower_half, rising[rows - 1 :], falling[:1])
            out_ref[i, p] = jnp.where(row_ids == 0, relaxed[o, p + 1], pltpu.roll(rising, 1, 0))
            out_ref[o, p] = jnp.where(
                row_ids == rows - 1, relaxed[i, p + 1], pltpu.roll(falling, rows - 1, 0)
            )
    rows_across = remote(6, row_send, row_recv, across)
    rows_across.start()
    for i in level_ids:
        for p in range(planes):
            out_ref[i, p] = carried(i, p)
    rows_across.wait()

    @pl.when(half == 0)
    def _():
        for j, i in enumerate(falling_ids):
            for p in range(planes):
                at = j * planes + p
                out_ref[i, p, rows - 1 :, :] = row_recv[at : at + 1, :]

    @pl.when(half != 0)
    def _():
        for j, i in enumerate(rising_ids):
            for p in range(planes):
                at = j * planes + p
                out_ref[i, p, :1, :] = row_recv[at : at + 1, :]


def shards(
    distributions, cell_states, cell_counts, up_list, down_list, spread_sites, stiffness, basis
):
    coefficients = cell_states.shape[2]
    capacity = cell_states.shape[3]
    planes, rows, columns = distributions.shape[1:]
    points, slots = spread_sites.shape
    move = up_list.shape[0]
    width = -(-coefficients // 128) * 128
    cells = jnp.pad(
        jnp.transpose(cell_states, (0, 1, 3, 2)),
        ((0, 0), (0, 0), (0, 0), (0, width - coefficients)),
    )
    scalars = pl.BlockSpec(memory_space=pltpu.SMEM)
    vectors = pl.BlockSpec(memory_space=pltpu.VMEM)
    f32 = jnp.float32
    new_distributions, moved = pl.pallas_call(
        step_kernel,
        out_shape=(
            jax.ShapeDtypeStruct(distributions.shape, f32),
            jax.ShapeDtypeStruct((2, 3, slots, width), f32),
        ),
        in_specs=[scalars] * 3 + [vectors] * 5,
        out_specs=(vectors, vectors),
        scratch_shapes=[
            pltpu.VMEM((width, points), f32),
            pltpu.VMEM((1, width), f32),
            pltpu.VMEM((3, slots, points), f32),
            pltpu.VMEM((6 * (planes + 2) * rows, columns), f32),
            pltpu.VMEM((2, 2, 3, move, width), f32),
            pltpu.VMEM((2, 2, 3, move, width), f32),
            pltpu.VMEM((2, 9, rows, columns), f32),
            pltpu.VMEM((2, 9, rows, columns), f32),
            pltpu.VMEM((2, 3, 2, rows, columns), f32),
            pltpu.VMEM((2, 3, 2, rows, columns), f32),
            pltpu.VMEM((16, columns), f32),
            pltpu.VMEM((16, columns), f32),
            pltpu.VMEM((4, planes, rows, columns), f32),
            pltpu.VMEM((19, planes + 2, rows, columns), f32),
            pltpu.SemaphoreType.DMA((7,)),
            pltpu.SemaphoreType.DMA((7,)),
        ],
        compiler_params=pltpu.CompilerParams(
            collective_id=0, has_side_effects=True, vmem_limit_bytes=48 * 1024 * 1024
        ),
    )(
        cell_counts,
        up_list,
        down_list,
        distributions,
        cells,
        spread_sites.T,
        stiffness.reshape(1, coefficients),
        basis,
    )
    moved_cells = jnp.transpose(moved[..., :coefficients], (0, 1, 3, 2))
    return (new_distributions, moved_cells)


def solution(mesh):
    placed = (
        P(None, "slab", "half", None),
        P(None, None, None, ("slab", "half")),
        P(("slab", "half")),
        P(("slab", "half")),
        P(("slab", "half")),
        P(None, ("slab", "half")),
        P(),
        P(),
    )
    return jax.shard_map(
        shards,
        mesh=mesh,
        in_specs=placed,
        out_specs=(P(None, "slab", "half", None), P(None, None, None, ("slab", "half"))),
        check_vma=False,
    )
```

```python
import jax
import jax.numpy as jnp
from jax import lax
from jax.experimental import pallas as pl
from jax.experimental.pallas import tpu as pltpu
from jax.sharding import PartitionSpec as P

full_precision = lax.Precision.HIGHEST
relaxation_time = 0.8
membrane_tension = 0.5
spread_weight = 0.05
lattice_velocities = (
    (0, 0, 0),
    (1, 0, 0),
    (-1, 0, 0),
    (0, 1, 0),
    (0, -1, 0),
    (0, 0, 1),
    (0, 0, -1),
    (1, 1, 0),
    (-1, -1, 0),
    (1, -1, 0),
    (-1, 1, 0),
    (1, 0, 1),
    (-1, 0, -1),
    (1, 0, -1),
    (-1, 0, 1),
    (0, 1, 1),
    (0, -1, -1),
    (0, 1, -1),
    (0, -1, 1),
)
lattice_weights = (1.0 / 3.0,) + (1.0 / 18.0,) * 6 + (1.0 / 36.0,) * 12
opposite_of = (0, 2, 1, 4, 3, 6, 5, 8, 7, 10, 9, 12, 11, 14, 13, 16, 15, 18, 17)
all_ids = tuple(range(19))
ahead_ids = tuple(i for i in all_ids if lattice_velocities[i][0] == 1)
behind_ids = tuple(i for i in all_ids if lattice_velocities[i][0] == -1)
rising_ids = tuple(i for i in all_ids if lattice_velocities[i][1] == 1)
falling_ids = tuple(opposite_of[i] for i in rising_ids)
level_ids = tuple(i for i in all_ids if lattice_velocities[i][1] == 0)


def total_of(terms):
    result = None
    for sign, value in terms:
        if sign == 0:
            continue
        if result is None:
            result = value if sign > 0 else -value
        else:
            result = result + value if sign > 0 else result - value
    return result


def moments_of(populations):
    density = total_of([(1, f) for f in populations])
    momentum = [
        total_of([(lattice_velocities[i][axis], populations[i]) for i in all_ids])
        for axis in range(3)
    ]
    return [density] + momentum


def collide(ids, population_of, moments, force):
    density = moments[0]
    inverse = 1.0 / density
    speed = [(moments[1 + a] + 0.5 * force[a]) * inverse for a in range(3)]
    speed_square = speed[0] * speed[0] + speed[1] * speed[1] + speed[2] * speed[2]
    power = speed[0] * force[0] + speed[1] * force[1] + speed[2] * force[2]
    base = 1.0 - 1.5 * speed_square
    result = {}
    for i in ids:
        vel = lattice_velocities[i]
        weight = lattice_weights[i]
        f = population_of(i)
        if i == 0:
            balance = (weight * density) * base
            source = (-3.0 * weight) * power
        else:
            projected = total_of(list(zip(vel, speed)))
            along = total_of(list(zip(vel, force)))
            balance = (weight * density) * (base + projected * (3.0 + 4.5 * projected))
            source = weight * (3.0 * (along - power) + 9.0 * projected * along)
        result[i] = (
            f - (f - balance) / relaxation_time + (1.0 - 0.5 / relaxation_time) * source
        )
    return result


def step_kernel(
    count_ref,
    up_in,
    down_in,
    dist_in,
    cells_in,
    sites_in,
    stiff_in,
    basis_in,
    out_ref,
    moved_out_ref,
    up_ref,
    down_ref,
    dist_ref,
    cells_ref,
    sites_ref,
    stiff_ref,
    basis_ref,
    load_sems,
    cells_by_slot,
    moved_ref,
    basis_pad,
    stiff_pad,
    pushes,
    spread_acc,
    cell_send,
    cell_recv,
    halo_send,
    halo_recv,
    force_own,
    force_recv,
    row_send,
    row_recv,
    own_moments,
    relaxed,
    send_sems,
    recv_sems,
):
    slab = lax.axis_index("slab")
    half = lax.axis_index("half")
    slabs = lax.axis_size("slab")
    above = {"slab": lax.rem(slab + 1, slabs), "half": half}
    below = {"slab": lax.rem(slab + slabs - 1, slabs), "half": half}
    across = {"slab": slab, "half": 1 - half}
    mesh_ids = pl.DeviceIdType.MESH

    planes, rows, columns = dist_ref.shape[1:]
    coefficients, points = basis_ref.shape
    capacity, width = cells_by_slot.shape[2:]
    move = up_ref.shape[0]
    slots = sites_ref.shape[0]
    padded_slots = moved_ref.shape[2]

    barrier = pltpu.get_barrier_semaphore()
    for device in (above, below, across):
        pl.semaphore_signal(barrier, inc=1, device_id=device, device_id_type=mesh_ids)

    loads = [
        pltpu.make_async_copy(source, target, load_sems.at[k])
        for k, (source, target) in enumerate(
            (
                (cells_in, cells_ref),
                (up_in, up_ref),
                (down_in, down_ref),
                (basis_in, basis_ref),
                (stiff_in, stiff_ref),
                (dist_in, dist_ref),
                (sites_in, sites_ref),
            )
        )
    ]
    for load in loads:
        load.start()

    def remote(at, source, target, device):
        return pltpu.make_async_remote_copy(
            src_ref=source,
            dst_ref=target,
            send_sem=send_sems.at[at],
            recv_sem=recv_sems.at[at],
            device_id=device,
            device_id_type=mesh_ids,
        )

    loads[0].wait()
    for w in range(2):
        for c in range(3):
            cells_by_slot[w, c] = jnp.pad(
                cells_ref[c, :, w, :],
                ((0, width - coefficients), (0, padded_slots - capacity)),
            ).T[:capacity]

    for load in loads[1:3]:
        load.wait()
    entry_ids = lax.broadcasted_iota(jnp.int32, (2 * move, capacity), 0)
    slot_ids = lax.broadcasted_iota(jnp.int32, (2 * move, capacity), 1)
    entries = jnp.zeros((2 * move, capacity), jnp.int32)
    for k in range(move):
        entries = jnp.where(entry_ids == k, up_ref[k], entries)
        entries = jnp.where(entry_ids == move + k, down_ref[k], entries)
    selector = (entries == slot_ids).astype(jnp.float32)
    for w in range(2):
        for c in range(3):
            picked = jnp.dot(
                selector,
                cells_by_slot[w, c],
                precision=full_precision,
                preferred_element_type=jnp.float32,
            )
            cell_send[0, w, c] = picked[:move]
            cell_send[1, w, c] = picked[move:]

    for load in loads[3:]:
        load.wait()
    for p in range(planes):
        moments = moments_of([dist_ref[i, p] for i in all_ids])
        for k in range(4):
            own_moments[k, p] = moments[k]
    for side, (p, ids) in enumerate(((planes - 1, ahead_ids), (0, behind_ids))):
        for k in range(4):
            halo_send[side, k] = own_moments[k, p]
        for k, i in enumerate(ids):
            halo_send[side, 4 + k] = dist_ref[i, p]
    basis_pad[...] = jnp.zeros_like(basis_pad)
    basis_pad[:coefficients, :] = basis_ref[...]
    stiff_pad[...] = jnp.zeros_like(stiff_pad)
    stiff_pad[:, :coefficients] = stiff_ref[...]

    held = lax.broadcasted_iota(jnp.int32, (capacity, width), 0)
    gone = held >= count_ref[0]
    for k in range(move):
        gone = gone | (held == up_ref[k]) | (held == down_ref[k])
    for w in range(2):
        for c in range(3):
            moved_ref[w, c, :capacity, :] = jnp.where(gone, 0.0, cells_by_slot[w, c])

    def point_forces(first, count):
        current = [moved_ref[0, c, first : first + count, :] for c in range(3)]
        rest = [moved_ref[1, c, first : first + count, :] for c in range(3)]
        stiffness = stiff_pad[...]
        strain = [stiffness * (r - x) for r, x in zip(rest, current)]
        product = jnp.dot(
            jnp.concatenate(current + strain, axis=0),
            basis_pad[...],
            precision=full_precision,
            preferred_element_type=jnp.float32,
        )
        parts = [product[k * count : (k + 1) * count] for k in range(6)]
        radial = [x - jnp.sum(x, axis=1, keepdims=True) / points for x in parts[:3]]
        squared = radial[0] * radial[0] + radial[1] * radial[1] + radial[2] * radial[2]
        mean_square = jnp.sum(squared, axis=1, keepdims=True) / points + 1e-05
        factor = membrane_tension * (squared / mean_square - 1.0)
        for c in range(3):
            pushes[c, first : first + count, :] = parts[3 + c] - factor * radial[c]

    group = 16
    site_rows = spread_acc.shape[0] // 6
    shift = columns.bit_length() - 1
    zero = jnp.zeros((), jnp.bfloat16)

    def spread(turn, carry):
        start = pl.multiple_of(turn * group, group)
        sites = sites_ref[pl.ds(start, group), :]
        row_of = (sites >> shift).astype(jnp.float32)
        column_of = (sites & (columns - 1)).astype(jnp.float32)
        values = []
        for c in range(3):
            push = pushes[c, pl.ds(start, group), :]
            coarse = push.astype(jnp.bfloat16).astype(jnp.float32)
            values += [coarse, push - coarse]
        row_ids = lax.broadcasted_iota(jnp.int32, (site_rows, points), 0)
        row_ids = row_ids.astype(jnp.float32).astype(jnp.bfloat16)
        column_ids = lax.broadcasted_iota(jnp.int32, (columns, points), 0)
        column_ids = column_ids.astype(jnp.float32).astype(jnp.bfloat16)

        def tall(array, k, height):
            tile = jnp.broadcast_to(array[k : k + 1], (16, points)).astype(jnp.bfloat16)
            return jnp.concatenate([tile] * (height // 16), axis=0)

        weighted = []
        hot = []
        for k in range(group):
            mask = row_ids == tall(row_of, k, site_rows)
            weighted.append(
                jnp.concatenate(
                    [jnp.where(mask, tall(v, k, site_rows), zero) for v in values], axis=0
                )
            )
            hot.append(
                jnp.where(
                    column_ids == tall(column_of, k, columns), jnp.ones((), jnp.bfloat16), zero
                )
            )
        spread_acc[...] += lax.dot_general(
            jnp.concatenate(weighted, axis=1),
            jnp.concatenate(hot, axis=1),
            (((1,), (1,)), ((), ())),
            preferred_element_type=jnp.float32,
        )
        return carry

    early = capacity // group // 3
    spread_acc[...] = jnp.zeros_like(spread_acc)
    point_forces(0, capacity)
    lax.fori_loop(0, early, spread, 0)

    pl.semaphore_wait(barrier, 3)
    cells_up = remote(0, cell_send.at[0], cell_recv.at[0], above)
    cells_down = remote(1, cell_send.at[1], cell_recv.at[1], below)
    cells_up.start()
    cells_down.start()

    halo_up = remote(2, halo_send.at[0], halo_recv.at[0], above)
    halo_down = remote(3, halo_send.at[1], halo_recv.at[1], below)
    halo_up.start()
    halo_down.start()

    lax.fori_loop(early, capacity // group, spread, 0)

    cells_up.wait()
    cells_down.wait()
    for w in range(2):
        for c in range(3):
            moved_ref[w, c, capacity : capacity + move, :] = cell_recv[0, w, c]
            moved_ref[w, c, capacity + move : slots, :] = cell_recv[1, w, c]
    point_forces(capacity, 2 * move)
    lax.fori_loop(capacity // group, slots // group, spread, 0)

    for c in range(3):
        first = 2 * c * site_rows
        whole = spread_acc[first : first + site_rows, :] + (
            spread_acc[first + site_rows : first + 2 * site_rows, :]
        )
        whole = (spread_weight * whole).reshape(2, 2, rows, columns)
        force_own[0, c] = whole[0]
        force_own[1, c] = whole[1]
    force_down = remote(4, force_own.at[0], force_recv.at[1], below)
    force_up = remote(5, force_own.at[1], force_recv.at[0], above)
    force_down.start()
    force_up.start()
    for w in range(2):
        for c in range(3):
            moved_out_ref[c, :, w, :] = moved_ref[w, c].T[:coefficients, :slots]
    halo_up.wait()
    halo_down.wait()
    force_down.wait()
    force_up.wait()

    for plane in range(planes + 2):
        side, at = divmod(plane, 2)
        force = [force_own[side, c, at] + force_recv[side, c, at] for c in range(3)]
        if plane == 0 or plane == planes + 1:
            which = 0 if plane == 0 else 1
            ids = ahead_ids if plane == 0 else behind_ids
            moments = [halo_recv[which, k] for k in range(4)]
            found = collide(
                ids, lambda i: halo_recv[which, 4 + ids.index(i)], moments, force
            )
        else:
            moments = [own_moments[k, plane - 1] for k in range(4)]
            found = collide(all_ids, lambda i: dist_ref[i, plane - 1], moments, force)
        for i, value in found.items():
            relaxed[i, plane] = value

    def carried(i, p):
        vel = lattice_velocities[i]
        value = relaxed[i, p + 1 - vel[0]]
        if vel[2]:
            value = pltpu.roll(value, vel[2] % columns, 1)
        return value

    row_ids = lax.broadcasted_iota(jnp.int32, (rows, columns), 0)
    lower_half = jnp.full((1, columns), half, jnp.int32) == 0
    for j, (i, o) in enumerate(zip(rising_ids, falling_ids)):
        for p in range(planes):
            rising = carried(i, p)
            falling = carried(o, p)
            at = j * planes + p
            row_send[at : at + 1, :] = jnp.where(lower_half, rising[rows - 1 :], falling[:1])
            out_ref[i, p] = jnp.where(row_ids == 0, relaxed[o, p + 1], pltpu.roll(rising, 1, 0))
            out_ref[o, p] = jnp.where(
                row_ids == rows - 1, relaxed[i, p + 1], pltpu.roll(falling, rows - 1, 0)
            )
    rows_across = remote(6, row_send, row_recv, across)
    rows_across.start()
    for i in level_ids:
        for p in range(planes):
            out_ref[i, p] = carried(i, p)
    rows_across.wait()

    @pl.when(half == 0)
    def _():
        for j, i in enumerate(falling_ids):
            for p in range(planes):
                at = j * planes + p
                out_ref[i, p, rows - 1 :, :] = row_recv[at : at + 1, :]

    @pl.when(half != 0)
    def _():
        for j, i in enumerate(rising_ids):
            for p in range(planes):
                at = j * planes + p
                out_ref[i, p, :1, :] = row_recv[at : at + 1, :]


def shards(
    distributions, cell_states, cell_counts, up_list, down_list, spread_sites, stiffness, basis
):
    coefficients = cell_states.shape[2]
    capacity = cell_states.shape[3]
    planes, rows, columns = distributions.shape[1:]
    points, slots = spread_sites.shape
    move = up_list.shape[0]
    width = -(-coefficients // 128) * 128
    padded_slots = -(-slots // 128) * 128
    anywhere = pl.BlockSpec(memory_space=pltpu.HBM)
    vectors = pl.BlockSpec(memory_space=pltpu.VMEM)
    f32 = jnp.float32
    new_distributions, moved = pl.pallas_call(
        step_kernel,
        out_shape=(
            pltpu.VMEM(distributions.shape, f32),
            pltpu.VMEM((3, coefficients, 2, slots), f32),
        ),
        in_specs=[pl.BlockSpec(memory_space=pltpu.SMEM)] + [anywhere] * 7,
        out_specs=(vectors, vectors),
        scratch_shapes=[
            pltpu.SMEM(up_list.shape, jnp.int32),
            pltpu.SMEM(down_list.shape, jnp.int32),
            pltpu.VMEM(distributions.shape, f32),
            pltpu.VMEM((3, coefficients, 2, capacity), f32),
            pltpu.VMEM((slots, points), jnp.int32),
            pltpu.VMEM((1, coefficients), f32),
            pltpu.VMEM((coefficients, points), f32),
            pltpu.SemaphoreType.DMA((7,)),
            pltpu.VMEM((2, 3, capacity, width), f32),
            pltpu.VMEM((2, 3, padded_slots, width), f32),
            pltpu.VMEM((width, points), f32),
            pltpu.VMEM((1, width), f32),
            pltpu.VMEM((3, slots, points), f32),
            pltpu.VMEM((6 * (planes + 2) * rows, columns), f32),
            pltpu.VMEM((2, 2, 3, move, width), f32),
            pltpu.VMEM((2, 2, 3, move, width), f32),
            pltpu.VMEM((2, 9, rows, columns), f32),
            pltpu.VMEM((2, 9, rows, columns), f32),
            pltpu.VMEM((2, 3, 2, rows, columns), f32),
            pltpu.VMEM((2, 3, 2, rows, columns), f32),
            pltpu.VMEM((16, columns), f32),
            pltpu.VMEM((16, columns), f32),
            pltpu.VMEM((4, planes, rows, columns), f32),
            pltpu.VMEM((19, planes + 2, rows, columns), f32),
            pltpu.SemaphoreType.DMA((7,)),
            pltpu.SemaphoreType.DMA((7,)),
        ],
        compiler_params=pltpu.CompilerParams(
            collective_id=0, has_side_effects=True, vmem_limit_bytes=56 * 1024 * 1024
        ),
    )(
        cell_counts,
        up_list,
        down_list,
        distributions,
        jnp.transpose(cell_states, (1, 2, 0, 3)),
        spread_sites.T,
        stiffness.reshape(1, coefficients),
        basis,
    )
    moved_cells = jnp.transpose(moved, (2, 0, 1, 3))
    return (new_distributions, moved_cells)


def solution(mesh):
    placed = (
        P(None, "slab", "half", None),
        P(None, None, None, ("slab", "half")),
        P(("slab", "half")),
        P(("slab", "half")),
        P(("slab", "half")),
        P(None, ("slab", "half")),
        P(),
        P(),
    )
    return jax.shard_map(
        shards,
        mesh=mesh,
        in_specs=placed,
        out_specs=(P(None, "slab", "half", None), P(None, None, None, ("slab", "half"))),
        check_vma=False,
    )
```

```python
import jax
import jax.numpy as jnp
from jax import lax
from jax.experimental import pallas as pl
from jax.experimental.pallas import tpu as pltpu
from jax.sharding import PartitionSpec as P

full_precision = lax.Precision.HIGHEST
relaxation_time = 0.8
membrane_tension = 0.5
spread_weight = 0.05
lattice_velocities = (
    (0, 0, 0),
    (1, 0, 0),
    (-1, 0, 0),
    (0, 1, 0),
    (0, -1, 0),
    (0, 0, 1),
    (0, 0, -1),
    (1, 1, 0),
    (-1, -1, 0),
    (1, -1, 0),
    (-1, 1, 0),
    (1, 0, 1),
    (-1, 0, -1),
    (1, 0, -1),
    (-1, 0, 1),
    (0, 1, 1),
    (0, -1, -1),
    (0, 1, -1),
    (0, -1, 1),
)
lattice_weights = (1.0 / 3.0,) + (1.0 / 18.0,) * 6 + (1.0 / 36.0,) * 12
opposite_of = (0, 2, 1, 4, 3, 6, 5, 8, 7, 10, 9, 12, 11, 14, 13, 16, 15, 18, 17)
all_ids = tuple(range(19))
ahead_ids = tuple(i for i in all_ids if lattice_velocities[i][0] == 1)
behind_ids = tuple(i for i in all_ids if lattice_velocities[i][0] == -1)
rising_ids = tuple(i for i in all_ids if lattice_velocities[i][1] == 1)
falling_ids = tuple(opposite_of[i] for i in rising_ids)
level_ids = tuple(i for i in all_ids if lattice_velocities[i][1] == 0)


def total_of(terms):
    result = None
    for sign, value in terms:
        if sign == 0:
            continue
        if result is None:
            result = value if sign > 0 else -value
        else:
            result = result + value if sign > 0 else result - value
    return result


def moments_of(populations):
    density = total_of([(1, f) for f in populations])
    momentum = [
        total_of([(lattice_velocities[i][axis], populations[i]) for i in all_ids])
        for axis in range(3)
    ]
    return [density] + momentum


def collide(ids, population_of, moments, force):
    density = moments[0]
    inverse = 1.0 / density
    speed = [(moments[1 + a] + 0.5 * force[a]) * inverse for a in range(3)]
    speed_square = speed[0] * speed[0] + speed[1] * speed[1] + speed[2] * speed[2]
    power = speed[0] * force[0] + speed[1] * force[1] + speed[2] * force[2]
    base = 1.0 - 1.5 * speed_square
    result = {}
    for i in ids:
        vel = lattice_velocities[i]
        weight = lattice_weights[i]
        f = population_of(i)
        if i == 0:
            balance = (weight * density) * base
            source = (-3.0 * weight) * power
        else:
            projected = total_of(list(zip(vel, speed)))
            along = total_of(list(zip(vel, force)))
            balance = (weight * density) * (base + projected * (3.0 + 4.5 * projected))
            source = weight * (3.0 * (along - power) + 9.0 * projected * along)
        result[i] = (
            f - (f - balance) / relaxation_time + (1.0 - 0.5 / relaxation_time) * source
        )
    return result


def step_kernel(
    count_ref,
    up_in,
    down_in,
    dist_in,
    cells_in,
    sites_in,
    stiff_in,
    basis_in,
    out_ref,
    moved_out_ref,
    up_ref,
    down_ref,
    dist_ref,
    cells_ref,
    sites_ref,
    stiff_ref,
    basis_ref,
    load_sems,
    cells_by_slot,
    moved_ref,
    basis_pad,
    stiff_pad,
    pushes,
    spread_acc,
    cell_send,
    cell_recv,
    halo_send,
    halo_recv,
    force_own,
    force_recv,
    row_send,
    row_recv,
    own_moments,
    relaxed,
    send_sems,
    recv_sems,
):
    slab = lax.axis_index("slab")
    half = lax.axis_index("half")
    slabs = lax.axis_size("slab")
    above = {"slab": lax.rem(slab + 1, slabs), "half": half}
    below = {"slab": lax.rem(slab + slabs - 1, slabs), "half": half}
    across = {"slab": slab, "half": 1 - half}
    mesh_ids = pl.DeviceIdType.MESH

    planes, rows, columns = dist_ref.shape[1:]
    coefficients, points = basis_ref.shape
    capacity, width = cells_by_slot.shape[2:]
    move = up_ref.shape[0]
    slots = sites_ref.shape[0]
    padded_slots = moved_ref.shape[2]

    barrier = pltpu.get_barrier_semaphore()
    for device in (above, below, across):
        pl.semaphore_signal(barrier, inc=1, device_id=device, device_id_type=mesh_ids)

    loads = [
        pltpu.make_async_copy(source, target, load_sems.at[k])
        for k, (source, target) in enumerate(
            (
                (cells_in, cells_ref),
                (up_in, up_ref),
                (down_in, down_ref),
                (basis_in, basis_ref),
                (stiff_in, stiff_ref),
                (dist_in, dist_ref),
                (sites_in, sites_ref),
            )
        )
    ]
    for load in loads:
        load.start()

    def remote(at, source, target, device):
        return pltpu.make_async_remote_copy(
            src_ref=source,
            dst_ref=target,
            send_sem=send_sems.at[at],
            recv_sem=recv_sems.at[at],
            device_id=device,
            device_id_type=mesh_ids,
        )

    loads[0].wait()
    for w in range(2):
        for c in range(3):
            cells_by_slot[w, c] = jnp.pad(
                cells_ref[c, :, w, :],
                ((0, width - coefficients), (0, padded_slots - capacity)),
            ).T[:capacity]

    for load in loads[1:3]:
        load.wait()
    entry_ids = lax.broadcasted_iota(jnp.int32, (2 * move, capacity), 0)
    slot_ids = lax.broadcasted_iota(jnp.int32, (2 * move, capacity), 1)
    entries = jnp.zeros((2 * move, capacity), jnp.int32)
    for k in range(move):
        entries = jnp.where(entry_ids == k, up_ref[k], entries)
        entries = jnp.where(entry_ids == move + k, down_ref[k], entries)
    selector = (entries == slot_ids).astype(jnp.float32)
    for w in range(2):
        for c in range(3):
            picked = jnp.dot(
                selector,
                cells_by_slot[w, c],
                precision=full_precision,
                preferred_element_type=jnp.float32,
            )
            cell_send[0, w, c] = picked[:move]
            cell_send[1, w, c] = picked[move:]

    for load in loads[3:]:
        load.wait()
    for p in range(planes):
        moments = moments_of([dist_ref[i, p] for i in all_ids])
        for k in range(4):
            own_moments[k, p] = moments[k]
    for side, (p, ids) in enumerate(((planes - 1, ahead_ids), (0, behind_ids))):
        for k in range(4):
            halo_send[side, k] = own_moments[k, p]
        for k, i in enumerate(ids):
            halo_send[side, 4 + k] = dist_ref[i, p]
    basis_pad[...] = jnp.zeros_like(basis_pad)
    basis_pad[:coefficients, :] = basis_ref[...]
    stiff_pad[...] = jnp.zeros_like(stiff_pad)
    stiff_pad[:, :coefficients] = stiff_ref[...]

    held = lax.broadcasted_iota(jnp.int32, (capacity, width), 0)
    gone = held >= count_ref[0]
    for k in range(move):
        gone = gone | (held == up_ref[k]) | (held == down_ref[k])
    for w in range(2):
        for c in range(3):
            moved_ref[w, c, :capacity, :] = jnp.where(gone, 0.0, cells_by_slot[w, c])

    def point_forces(first, count):
        current = [moved_ref[0, c, first : first + count, :] for c in range(3)]
        rest = [moved_ref[1, c, first : first + count, :] for c in range(3)]
        stiffness = stiff_pad[...]
        strain = [stiffness * (r - x) for r, x in zip(rest, current)]
        product = jnp.dot(
            jnp.concatenate(current + strain, axis=0),
            basis_pad[...],
            precision=full_precision,
            preferred_element_type=jnp.float32,
        )
        parts = [product[k * count : (k + 1) * count] for k in range(6)]
        radial = [x - jnp.sum(x, axis=1, keepdims=True) / points for x in parts[:3]]
        squared = radial[0] * radial[0] + radial[1] * radial[1] + radial[2] * radial[2]
        mean_square = jnp.sum(squared, axis=1, keepdims=True) / points + 1e-05
        factor = membrane_tension * (squared / mean_square - 1.0)
        for c in range(3):
            pushes[c, first : first + count, :] = parts[3 + c] - factor * radial[c]

    group = 16
    site_rows = spread_acc.shape[0] // 6
    shift = columns.bit_length() - 1
    zero = jnp.zeros((), jnp.bfloat16)

    def spread(turn, carry):
        start = pl.multiple_of(turn * group, group)
        sites = sites_ref[pl.ds(start, group), :]
        row_of = (sites >> shift).astype(jnp.float32)
        column_of = (sites & (columns - 1)).astype(jnp.float32)
        values = []
        for c in range(3):
            push = pushes[c, pl.ds(start, group), :]
            coarse = push.astype(jnp.bfloat16).astype(jnp.float32)
            values += [coarse, push - coarse]
        row_ids = lax.broadcasted_iota(jnp.int32, (site_rows, points), 0)
        row_ids = row_ids.astype(jnp.float32).astype(jnp.bfloat16)
        column_ids = lax.broadcasted_iota(jnp.int32, (columns, points), 0)
        column_ids = column_ids.astype(jnp.float32).astype(jnp.bfloat16)

        def tall(array, k, height):
            tile = jnp.broadcast_to(array[k : k + 1], (16, points)).astype(jnp.bfloat16)
            return jnp.concatenate([tile] * (height // 16), axis=0)

        weighted = []
        hot = []
        for k in range(group):
            mask = row_ids == tall(row_of, k, site_rows)
            weighted.append(
                jnp.concatenate(
                    [jnp.where(mask, tall(v, k, site_rows), zero) for v in values], axis=0
                )
            )
            hot.append(
                jnp.where(
                    column_ids == tall(column_of, k, columns), jnp.ones((), jnp.bfloat16), zero
                )
            )
        spread_acc[...] += lax.dot_general(
            jnp.concatenate(weighted, axis=1),
            jnp.concatenate(hot, axis=1),
            (((1,), (1,)), ((), ())),
            preferred_element_type=jnp.float32,
        )
        return carry

    early = capacity // group // 3
    spread_acc[...] = jnp.zeros_like(spread_acc)
    point_forces(0, capacity)
    lax.fori_loop(0, early, spread, 0)

    pl.semaphore_wait(barrier, 3)
    cells_up = remote(0, cell_send.at[0], cell_recv.at[0], above)
    cells_down = remote(1, cell_send.at[1], cell_recv.at[1], below)
    cells_up.start()
    cells_down.start()

    halo_up = remote(2, halo_send.at[0], halo_recv.at[0], above)
    halo_down = remote(3, halo_send.at[1], halo_recv.at[1], below)
    halo_up.start()
    halo_down.start()

    lax.fori_loop(early, capacity // group, spread, 0)

    cells_up.wait()
    cells_down.wait()
    for w in range(2):
        for c in range(3):
            moved_ref[w, c, capacity : capacity + move, :] = cell_recv[0, w, c]
            moved_ref[w, c, capacity + move : slots, :] = cell_recv[1, w, c]
    point_forces(capacity, 2 * move)
    lax.fori_loop(capacity // group, slots // group, spread, 0)

    for c in range(3):
        first = 2 * c * site_rows
        whole = spread_acc[first : first + site_rows, :] + (
            spread_acc[first + site_rows : first + 2 * site_rows, :]
        )
        whole = (spread_weight * whole).reshape(2, 2, rows, columns)
        force_own[0, c] = whole[0]
        force_own[1, c] = whole[1]
    force_down = remote(4, force_own.at[0], force_recv.at[1], below)
    force_up = remote(5, force_own.at[1], force_recv.at[0], above)
    force_down.start()
    force_up.start()
    for w in range(2):
        for c in range(3):
            moved_out_ref[c, :, w, :] = moved_ref[w, c].T[:coefficients, :slots]
    halo_up.wait()
    halo_down.wait()
    force_down.wait()
    force_up.wait()

    def collided(plane, ids, span):
        side, at = divmod(plane, 2)
        force = [
            force_own[side, c, at, span, :] + force_recv[side, c, at, span, :] for c in range(3)
        ]
        if plane == 0 or plane == planes + 1:
            which = 0 if plane == 0 else 1
            sent = ahead_ids if plane == 0 else behind_ids
            ids = [i for i in ids if i in sent]
            moments = [halo_recv[which, k, span, :] for k in range(4)]
            return collide(
                ids, lambda i: halo_recv[which, 4 + sent.index(i), span, :], moments, force
            )
        moments = [own_moments[k, plane - 1, span, :] for k in range(4)]
        return collide(ids, lambda i: dist_ref[i, plane - 1, span, :], moments, force)

    border = pl.ds(pl.multiple_of((1 - half) * (rows - 8), 8), 8)
    lower_half = jnp.full((1, columns), half, jnp.int32) == 0
    edge = [collided(plane, rising_ids + falling_ids, border) for plane in range(planes + 2)]

    def edge_row(i, p, at):
        vel = lattice_velocities[i]
        value = edge[p + 1 - vel[0]][i]
        if vel[2]:
            value = pltpu.roll(value, vel[2] % columns, 1)
        return value[at : at + 1]

    for j, (i, o) in enumerate(zip(rising_ids, falling_ids)):
        for p in range(planes):
            at = j * planes + p
            row_send[at : at + 1, :] = jnp.where(lower_half, edge_row(i, p, 7), edge_row(o, p, 0))
    rows_across = remote(6, row_send, row_recv, across)
    rows_across.start()

    for plane in range(planes + 2):
        for i, value in collided(plane, all_ids, slice(0, rows)).items():
            relaxed[i, plane] = value

    def carried(i, p):
        vel = lattice_velocities[i]
        value = relaxed[i, p + 1 - vel[0]]
        if vel[2]:
            value = pltpu.roll(value, vel[2] % columns, 1)
        return value

    row_ids = lax.broadcasted_iota(jnp.int32, (rows, columns), 0)
    for j, (i, o) in enumerate(zip(rising_ids, falling_ids)):
        for p in range(planes):
            rising = carried(i, p)
            falling = carried(o, p)
            out_ref[i, p] = jnp.where(row_ids == 0, relaxed[o, p + 1], pltpu.roll(rising, 1, 0))
            out_ref[o, p] = jnp.where(
                row_ids == rows - 1, relaxed[i, p + 1], pltpu.roll(falling, rows - 1, 0)
            )
    for i in level_ids:
        for p in range(planes):
            out_ref[i, p] = carried(i, p)
    rows_across.wait()

    @pl.when(half == 0)
    def _():
        for j, i in enumerate(falling_ids):
            for p in range(planes):
                at = j * planes + p
                out_ref[i, p, rows - 1 :, :] = row_recv[at : at + 1, :]

    @pl.when(half != 0)
    def _():
        for j, i in enumerate(rising_ids):
            for p in range(planes):
                at = j * planes + p
                out_ref[i, p, :1, :] = row_recv[at : at + 1, :]


def shards(
    distributions, cell_states, cell_counts, up_list, down_list, spread_sites, stiffness, basis
):
    coefficients = cell_states.shape[2]
    capacity = cell_states.shape[3]
    planes, rows, columns = distributions.shape[1:]
    points, slots = spread_sites.shape
    move = up_list.shape[0]
    width = -(-coefficients // 128) * 128
    padded_slots = -(-slots // 128) * 128
    anywhere = pl.BlockSpec(memory_space=pltpu.HBM)
    vectors = pl.BlockSpec(memory_space=pltpu.VMEM)
    f32 = jnp.float32
    new_distributions, moved = pl.pallas_call(
        step_kernel,
        out_shape=(
            pltpu.VMEM(distributions.shape, f32),
            pltpu.VMEM((3, coefficients, 2, slots), f32),
        ),
        in_specs=[pl.BlockSpec(memory_space=pltpu.SMEM)] + [anywhere] * 7,
        out_specs=(vectors, vectors),
        scratch_shapes=[
            pltpu.SMEM(up_list.shape, jnp.int32),
            pltpu.SMEM(down_list.shape, jnp.int32),
            pltpu.VMEM(distributions.shape, f32),
            pltpu.VMEM((3, coefficients, 2, capacity), f32),
            pltpu.VMEM((slots, points), jnp.int32),
            pltpu.VMEM((1, coefficients), f32),
            pltpu.VMEM((coefficients, points), f32),
            pltpu.SemaphoreType.DMA((7,)),
            pltpu.VMEM((2, 3, capacity, width), f32),
            pltpu.VMEM((2, 3, padded_slots, width), f32),
            pltpu.VMEM((width, points), f32),
            pltpu.VMEM((1, width), f32),
            pltpu.VMEM((3, slots, points), f32),
            pltpu.VMEM((6 * (planes + 2) * rows, columns), f32),
            pltpu.VMEM((2, 2, 3, move, width), f32),
            pltpu.VMEM((2, 2, 3, move, width), f32),
            pltpu.VMEM((2, 9, rows, columns), f32),
            pltpu.VMEM((2, 9, rows, columns), f32),
            pltpu.VMEM((2, 3, 2, rows, columns), f32),
            pltpu.VMEM((2, 3, 2, rows, columns), f32),
            pltpu.VMEM((16, columns), f32),
            pltpu.VMEM((16, columns), f32),
            pltpu.VMEM((4, planes, rows, columns), f32),
            pltpu.VMEM((19, planes + 2, rows, columns), f32),
            pltpu.SemaphoreType.DMA((7,)),
            pltpu.SemaphoreType.DMA((7,)),
        ],
        compiler_params=pltpu.CompilerParams(
            collective_id=0, has_side_effects=True, vmem_limit_bytes=56 * 1024 * 1024
        ),
    )(
        cell_counts,
        up_list,
        down_list,
        distributions,
        jnp.transpose(cell_states, (1, 2, 0, 3)),
        spread_sites.T,
        stiffness.reshape(1, coefficients),
        basis,
    )
    moved_cells = jnp.transpose(moved, (2, 0, 1, 3))
    return (new_distributions, moved_cells)


def solution(mesh):
    placed = (
        P(None, "slab", "half", None),
        P(None, None, None, ("slab", "half")),
        P(("slab", "half")),
        P(("slab", "half")),
        P(("slab", "half")),
        P(None, ("slab", "half")),
        P(),
        P(),
    )
    return jax.shard_map(
        shards,
        mesh=mesh,
        in_specs=placed,
        out_specs=(P(None, "slab", "half", None), P(None, None, None, ("slab", "half"))),
        check_vma=False,
    )
```
